32 devices in a mesh: node: 4 (over y, core), local: 8 (over z, x).
Axes of the slice: x: 2, y: 2, z: 4, core: 2. Of those that a mesh axis runs over, the one named last changes fastest.
Arguments:
- tokens: bfloat16 [2048, 3584], P(('node', 'local')), may hold values from -6 to 6
- expert_ids: int32 [2048, 8], P(('node', 'local')), may hold values from 0 to 31, as said below
- gate_values: bfloat16 [2048, 8], P(('node', 'local')), may hold values from 0.049804688 to 0.44921875
- expert_gate: bfloat16 [32, 3584, 1024], P(('node', 'local')), may hold values from -0.09375 to 0.09375
- expert_up: bfloat16 [32, 3584, 1024], P(('node', 'local')), may hold values from -0.09375 to 0.09375
- expert_down: bfloat16 [32, 1024, 3584], P(('node', 'local')), may hold values from -0.1875 to 0.1875
Outputs:
- mixed: bfloat16 [2048, 3584], P(('node', 'local'))
The draws below stay inside these ranges and needn't reach their ends.
Inputs may be any that keep to these rules, and one draw needn't show every extreme that they name: `expert_ids`: each row names 8 different experts, the same number on each of exactly 4 nodes. Among the rows of one device, each node is named by exactly 64 rows, no expert is named more than 32 times, and on every node some expert is named exactly 32 times.
All inputs are finite; a program needn't handle non-finite values.
Results may differ from the reference program's by a relative error of at most 0.012.
Values may be sent and summed in bfloat16 or wider, within the bound.
A program may use at most 128 MiB of HBM per device.

```python
import jax
import jax.numpy as jnp
from jax import lax

D = 3584
FF = 1024
TOPK = 8
NODES_HIT = 4
TOK_DEV = 64
EXPERTS = 32
CAP = 32
TOKENS = 2048
N_NODE = 4
N_LOCAL = 8


def route_block(block_key):
    band = TOK_DEV // N_NODE
    pair = TOPK // NODES_HIT
    key_nodes, key_place, key_local = jax.random.split(block_key, 3)
    node_order = jax.random.permutation(key_nodes, N_NODE).astype(jnp.int32)
    token_place = jax.random.permutation(key_place, TOK_DEV).astype(jnp.int32)
    local_keys = jax.random.split(key_local, N_NODE)
    local_orders = jax.vmap(lambda k: jax.random.permutation(k, N_LOCAL).astype(jnp.int32))(local_keys)
    start = token_place % N_NODE
    band_index = token_place // N_NODE
    window = jnp.arange(NODES_HIT, dtype=jnp.int32)
    slot_node = (start[:, None] + window[None, :]) % N_NODE
    rank = window[None, :] * band + band_index[:, None]
    busy = rank < CAP
    others = N_LOCAL - 1
    stream = CAP + 2 * (rank - CAP)
    first = jnp.where(busy, 0, 1 + stream % others)
    second = jnp.where(busy, 1 + rank % others, 1 + (stream + 1) % others)
    orders = local_orders[slot_node]
    local_a = jnp.take_along_axis(orders, first[:, :, None], axis=2)[:, :, 0]
    local_b = jnp.take_along_axis(orders, second[:, :, None], axis=2)[:, :, 0]
    node = node_order[slot_node]
    chosen = jnp.stack([node * N_LOCAL + local_a, node * N_LOCAL + local_b], axis=2)
    return chosen.reshape(TOK_DEV, NODES_HIT * pair).astype(jnp.int32)


def draw_expert_ids(key, part):
    key = jax.random.fold_in(key, 11)
    block_keys = jax.random.split(key, TOKENS // TOK_DEV)
    blocks = jax.vmap(route_block)(block_keys)
    return blocks.reshape(TOKENS, TOPK).astype(jnp.int32)


def steps_of(stream_key, shape, shards, smallest, top_value):
    loudness = 1.0
    for dim, shards_of in shards:
        steps = jax.random.uniform(jax.random.fold_in(jax.random.fold_in(stream_key, 6), dim), (shards_of,), jnp.float32, smallest / len(shards), top_value / len(shards))
        loudness = loudness * jnp.repeat(jnp.exp(steps), shape[dim] // shards_of).reshape((-1,) + (1,) * (len(shape) - 1 - dim))
    return loudness


def gaussian(stream_key, dims, scale, most, pieces=(), kind=jnp.bfloat16):
    factor_of = steps_of(stream_key, dims, pieces, -0.22, 0.18) if pieces else 1.0
    drawn = jax.random.normal(stream_key, dims, jnp.float32) * scale * factor_of
    return jnp.minimum(jnp.maximum(drawn, -most), most).astype(kind)


def setup_inputs(seed: int = 0) -> dict:
    arg_keys = jax.random.split(jax.random.key(seed), 7)
    return {
        "tokens": gaussian(arg_keys[0], (TOKENS, D), 1.0, 6.0, ((0, 32),)),
        "expert_ids": draw_expert_ids(jax.random.fold_in(arg_keys[6], 71), 0),
        "gate_values": jnp.clip(0.049804688 + 0.39941406 * jax.random.uniform(arg_keys[2], (TOKENS, TOPK), jnp.float32) ** steps_of(arg_keys[2], (TOKENS, TOPK), ((0, 32),), -0.2, 0.2), 0.049804688, 0.44921875).astype(jnp.bfloat16),
        "expert_gate": gaussian(arg_keys[3], (EXPERTS, D, FF), D ** -0.5, 0.09375, ((0, 32),)),
        "expert_up": gaussian(arg_keys[4], (EXPERTS, D, FF), D ** -0.5, 0.09375, ((0, 32),)),
        "expert_down": gaussian(arg_keys[5], (EXPERTS, FF, D), FF ** -0.5, 0.1875, ((0, 32),)),
    }


def expert_apply(rows, w_gate, w_up, w_down):
    gate_rows = jnp.dot(rows, w_gate, preferred_element_type=jnp.float32)
    up_rows = jnp.dot(rows, w_up, preferred_element_type=jnp.float32)
    hidden = (jax.nn.silu(gate_rows) * up_rows).astype(jnp.bfloat16)
    return jnp.dot(hidden, w_down, preferred_element_type=jnp.float32).astype(jnp.bfloat16)


def reference(tokens, expert_ids, gate_values, expert_gate, expert_up, expert_down):
    room = EXPERTS * CAP
    flat_ids = expert_ids.reshape(-1).astype(jnp.int32)
    order = jnp.argsort(flat_ids, stable=True).astype(jnp.int32)
    counts = jnp.bincount(flat_ids, length=EXPERTS).astype(jnp.int32)
    starts = (jnp.cumsum(counts) - counts).astype(jnp.int32)
    padded_order = jnp.concatenate([order, jnp.zeros((room,), jnp.int32)])
    gates_flat = gate_values.reshape(-1).astype(jnp.float32)
    positions = jnp.arange(room, dtype=jnp.int32)

    def node_sum(node):
        def step(total, local):
            expert = (node * N_LOCAL + local).astype(jnp.int32)
            picked = lax.dynamic_slice(padded_order, (starts[expert].astype(jnp.int32),), (room,))
            live = positions < counts[expert]
            token_index = (picked // TOPK).astype(jnp.int32)
            outputs = expert_apply(tokens[token_index], expert_gate[expert], expert_up[expert], expert_down[expert])
            weight = jnp.where(live, gates_flat[picked], jnp.float32(0.0))
            total = total.at[token_index].add(weight[:, None] * outputs.astype(jnp.float32))
            return total, None

        start = jnp.zeros((TOKENS, D), jnp.float32)
        total, _ = lax.scan(step, start, jnp.arange(N_LOCAL, dtype=jnp.int32))
        rounded = lax.optimization_barrier(total.astype(jnp.bfloat16))
        return rounded.astype(jnp.float32)

    def add_node(node, mixed_sum):
        return mixed_sum + node_sum(jnp.int32(node))

    mixed_sum = lax.fori_loop(0, N_NODE, add_node, jnp.zeros((TOKENS, D), jnp.float32))
    return mixed_sum.astype(jnp.bfloat16)
```

```python
import functools

import jax
import jax.numpy as jnp
from jax import lax
from jax.experimental import pallas as pl
from jax.experimental.pallas import tpu as pltpu
from jax.sharding import PartitionSpec as P

BF16 = jnp.bfloat16
F32 = jnp.float32
LANES = 128


def expert_rows(rows, w_gate, w_up, w_down):
    shape = rows.shape
    flat = rows.reshape(-1, shape[-1])
    gate_rows = jnp.dot(flat, w_gate, preferred_element_type=jnp.float32)
    up_rows = jnp.dot(flat, w_up, preferred_element_type=jnp.float32)
    hidden = (jax.nn.silu(gate_rows) * up_rows).astype(jnp.bfloat16)
    output = jnp.dot(hidden, w_down, preferred_element_type=jnp.float32).astype(jnp.bfloat16)
    return output.reshape(shape)


def shards_all_to_all(tokens, expert_ids, gate_values, expert_gate, expert_up, expert_down):
    nodes = lax.axis_size("node")
    per_node = lax.axis_size("local")
    experts = nodes * per_node
    tok_rows, width = tokens.shape
    top = expert_ids.shape[1]
    cap = 2 * tok_rows * top // experts
    w_gate = expert_gate[0]
    w_up = expert_up[0]
    w_down = expert_down[0]
    hits = (expert_ids[:, :, None] == jnp.arange(experts, dtype=jnp.int32)[None, None, :]).astype(
        jnp.int32
    )
    flat_hits = hits.reshape(tok_rows * top, experts)
    earlier = jnp.cumsum(flat_hits, axis=0) - flat_hits
    slot = jnp.sum(earlier * flat_hits, axis=1).reshape(tok_rows, top)
    position = expert_ids * cap + slot
    places = jnp.arange(experts * cap, dtype=jnp.int32)
    chosen = places[:, None, None] == position[None, :, :]
    dispatch = jnp.any(chosen, axis=2).astype(jnp.bfloat16)
    weights = jnp.sum(
        jnp.where(chosen, gate_values[None, :, :].astype(jnp.float32), jnp.float32(0.0)), axis=2
    )
    send = jnp.dot(dispatch, tokens, preferred_element_type=jnp.float32).astype(jnp.bfloat16)
    back = lax.all_to_all(
        expert_rows(
            lax.all_to_all(
                send.reshape(experts, cap, width),
                ("node", "local"),
                split_axis=0,
                concat_axis=0,
                tiled=True,
            ),
            w_gate,
            w_up,
            w_down,
        ),
        ("node", "local"),
        split_axis=0,
        concat_axis=0,
        tiled=True,
    )
    mix = weights.astype(jnp.bfloat16).reshape(nodes, per_node * cap, tok_rows)
    node_part = jnp.einsum(
        "nct,ncd->ntd",
        mix,
        back.reshape(nodes, per_node * cap, width),
        preferred_element_type=jnp.float32,
    ).astype(jnp.bfloat16)
    return jnp.sum(node_part.astype(jnp.float32), axis=0).astype(jnp.bfloat16)


def fused(
    spots,
    experts,
    cap,
    tok_ref,
    ids_ref,
    gates_ref,
    gate_hbm,
    up_hbm,
    down_hbm,
    out_ref,
    held,
    mine,
    from_core,
    from_second,
    from_first,
    from_line,
    w_gate,
    w_up,
    w_down,
    rows,
    hidden,
    pick,
    blend,
    local_sem,
    line_s,
    line_r,
    first_s,
    first_r,
    second_s,
    second_r,
    core_s,
    core_r,
    back_core_s,
    back_core_r,
    back_second_s,
    back_second_r,
    back_first_s,
    back_first_r,
    back_line_s,
    back_line_r,
):
    tok_rows, width = tok_ref.shape
    ff = w_gate.shape[1]
    quad = 4 * tok_rows
    slots = 4 * cap
    node = lax.axis_index("node")
    local = lax.axis_index("local")
    expert = node * (2 * spots) + local
    y, c, z, x = node // 2, node % 2, local // 2, local % 2
    a, b = x + c * (y - x), y + c * (x - y)
    step_a, step_b = 1 + c, 2 - c

    def q(i, j):
        return i * step_a + j * step_b

    def q_core(i, j):
        return i * step_b + j * step_a

    own = q(a, b)
    order = ((a, b), (1 - a, b), (a, 1 - b), (1 - a, 1 - b))
    order_core = ((b, a), (1 - b, a), (b, 1 - a), (1 - b, 1 - a))
    first = ((y + c * (1 - 2 * y)) * 2 + c, z * 2 + x + (1 - c) * (1 - 2 * x))
    second = ((y + (1 - c) * (1 - 2 * y)) * 2 + c, z * 2 + x + c * (1 - 2 * x))
    sibling = (y * 2 + 1 - c, local)

    def along(k):
        return (node, ((z + k) % spots) * 2 + x)

    def spot(k):
        return (z + spots - k) % spots

    barrier = pltpu.get_barrier_semaphore()
    partners = [first, second, sibling] + [along(k) for k in range(1, spots)]
    for partner in partners:
        pl.semaphore_signal(
            barrier, inc=1, device_id=partner, device_id_type=pl.DeviceIdType.MESH
        )

    loads = [
        pltpu.make_async_copy(tok_ref, mine.at[:, pl.ds(0, width)], local_sem.at[0]),
        pltpu.make_async_copy(gate_hbm.at[0], w_gate, local_sem.at[1]),
        pltpu.make_async_copy(up_hbm.at[0], w_up, local_sem.at[2]),
        pltpu.make_async_copy(down_hbm.at[0], w_down, local_sem.at[3]),
    ]
    for load in loads:
        load.start()

    lane = lax.broadcasted_iota(jnp.int32, (tok_rows, LANES), 1)
    weight = jnp.zeros((tok_rows, LANES), F32)
    hit = jnp.zeros((tok_rows, LANES), F32)
    for k in range(ids_ref.shape[1]):
        chosen = ids_ref[:, k : k + 1]
        value = gates_ref[:, k : k + 1].astype(F32)
        weight = weight + jnp.where(lane == chosen, value, 0.0)
        hit = hit + jnp.where(lane == chosen + experts, 1.0, 0.0)
    earlier = (
        lax.broadcasted_iota(jnp.int32, (tok_rows, tok_rows), 0)
        > lax.broadcasted_iota(jnp.int32, (tok_rows, tok_rows), 1)
    )
    before = jnp.dot(
        jnp.where(earlier, 1.0, 0.0).astype(BF16), hit.astype(BF16), preferred_element_type=F32
    )
    mine[:, pl.ds(width, LANES)] = (weight + hit * (before + 1.0)).astype(BF16)
    loads[0].wait()
    keep = pltpu.make_async_copy(mine, held.at[z, c, own], local_sem.at[4])
    keep.start()
    pl.semaphore_wait(barrier, len(partners))

    def send(src, dst, send_sem, recv_sem, device):
        return pltpu.make_async_remote_copy(
            src_ref=src,
            dst_ref=dst,
            send_sem=send_sem,
            recv_sem=recv_sem,
            device_id=device,
            device_id_type=pl.DeviceIdType.MESH,
        )

    def block(k, i):
        return held.at[spot(k), c, q(*order[i])]

    def source(k, i):
        return mine if k == 0 and i == 0 else block(k, i)

    def to_line(k):
        return send(mine, held.at[z, c, own], line_s.at[k - 1], line_r.at[k - 1], along(k))

    def to_first(k):
        return send(source(k, 0), block(k, 0), first_s.at[k], first_r.at[k], first)

    def to_second(k, i):
        return send(source(k, i), block(k, i), second_s.at[k, i], second_r.at[k, i], second)

    def to_core(k, i):
        return send(source(k, i), block(k, i), core_s.at[k, i], core_r.at[k, i], sibling)

    def gather_a(k):
        if k > 0:
            send(mine, block(k, 0), line_s.at[k - 1], line_r.at[k - 1], along(k)).wait_recv()
        to_first(k).start()
        to_second(k, 0).start()
        to_core(k, 0).start()
        if k == 0:
            for hop in range(1, spots):
                to_line(hop).start()

    def gather_b(k):
        send(mine, block(k, 1), first_s.at[k], first_r.at[k], first).wait_recv()
        to_second(k, 1).start()
        to_core(k, 1).start()

    def gather_c(k):
        for i in range(2):
            send(
                mine, block(k, 2 + i), second_s.at[k, i], second_r.at[k, i], second
            ).wait_recv()
            to_core(k, 2 + i).start()

    def gather_d(k):
        for i in range(4):
            place = held.at[spot(k), 1 - c, q_core(*order_core[i])]
            send(mine, place, core_s.at[k, i], core_r.at[k, i], sibling).wait_recv()

    def gather_sent(k):
        to_first(k).wait_send()
        for i in range(2):
            to_second(k, i).wait_send()
        for i in range(4):
            to_core(k, i).wait_send()

    def dispatch(k):
        s = spot(k)
        lane = lax.broadcasted_iota(jnp.int32, (quad, LANES), 1)
        base = (lax.broadcasted_iota(jnp.int32, (quad, 1), 0) // tok_rows * cap).astype(F32)
        column = lax.broadcasted_iota(jnp.int32, (quad, slots), 1).astype(F32)
        for h in range(2):
            notes = held[s, h, :, :, pl.ds(width, LANES)].reshape(quad, LANES).astype(F32)
            weight = jnp.sum(jnp.where(lane == expert, notes, 0.0), axis=1, keepdims=True)
            place = jnp.sum(
                jnp.where(lane == expert + experts, notes, 0.0), axis=1, keepdims=True
            )
            target = jnp.where(place > 0.0, place - 1.0 + base, -1.0)
            pick[h] = jnp.where(column == target, 1.0, 0.0).astype(BF16)
            blend[h] = jnp.where(column == target, weight, 0.0).astype(BF16)

        def piece(j, carry):
            cols = pl.ds(pl.multiple_of(j * 512, 512), 512)
            for h in range(2):
                rows[pl.ds(h * slots, slots), cols] = lax.dot_general(
                    pick[h],
                    held[s, h, :, :, cols].reshape(quad, 512),
                    (((0,), (0,)), ((), ())),
                    preferred_element_type=F32,
                ).astype(BF16)
            return carry

        lax.fori_loop(0, width // 512, piece, 0)

    def expand(k):
        if k == 0:
            loads[1].wait()
            loads[2].wait()

        def piece(j, carry):
            cols = pl.ds(pl.multiple_of(j * 256, 256), 256)
            gate = jnp.dot(rows[...], w_gate[:, cols], preferred_element_type=F32)
            up = jnp.dot(rows[...], w_up[:, cols], preferred_element_type=F32)
            hidden[:, cols] = (gate / (1.0 + jnp.exp(-gate)) * up).astype(BF16)
            return carry

        lax.fori_loop(0, ff // 256, piece, 0)

    def contract(k):
        s = spot(k)
        if k == 0:
            loads[3].wait()
        gather_sent(k)

        def piece(j, carry):
            cols = pl.ds(pl.multiple_of(j * 512, 512), 512)
            made = jnp.dot(hidden[...], w_down[:, cols], preferred_element_type=F32).astype(BF16)
            for h in range(2):
                held[s, h, :, :, cols] = (
                    jnp.dot(
                        blend[h], made[h * slots : (h + 1) * slots], preferred_element_type=F32
                    )
                    .astype(BF16)
                    .reshape(4, tok_rows, 512)
                )
            return carry

        lax.fori_loop(0, width // 512, piece, 0)

    features = pl.ds(0, width)

    def back_core(k):
        return send(
            held.at[spot(k), 1 - c, :, :, features],
            from_core.at[k],
            back_core_s.at[k],
            back_core_r.at[k],
            sibling,
        )

    def back_second(k, i):
        return send(
            held.at[spot(k), c, q(i, 1 - b), :, features],
            from_second.at[k, i],
            back_second_s.at[k, i],
            back_second_r.at[k, i],
            second,
        )

    def back_first(k):
        return send(
            held.at[spot(k), c, q(1 - a, b), :, features],
            from_first.at[k],
            back_first_s.at[k],
            back_first_r.at[k],
            first,
        )

    def back_line(k):
        return send(
            held.at[spot(k), c, own, :, features],
            from_line.at[k - 1],
            back_line_s.at[k - 1],
            back_line_r.at[k - 1],
            (node, spot(k) * 2 + x),
        )

    def add(k, place, other):
        held[spot(k), c, place, :, features] = (
            held[spot(k), c, place, :, features].astype(F32) + other.astype(F32)
        ).astype(BF16)

    def back_1(k):
        back_core(k).start()

    def back_2(k):
        back_core(k).wait_recv()
        for i in range(2):
            add(k, q(i, 1 - b), from_core[k, q(i, 1 - b)])
            back_second(k, i).start()
        for i in range(2):
            add(k, q(i, b), from_core[k, q(i, b)])

    def back_3(k):
        back_second(k, 0).wait_recv()
        back_second(k, 1).wait_recv()
        add(k, q(1 - a, b), from_second[k, 1 - a])
        back_first(k).start()
        add(k, own, from_second[k, a])

    def back_4(k):
        back_first(k).wait_recv()
        add(k, own, from_first[k])
        if k > 0:
            back_line(k).start()

    gather_a(0)
    gather_b(0)
    gather_a(1)
    gather_c(0)
    gather_b(1)
    gather_d(0)
    keep.wait()
    dispatch(0)
    expand(0)
    gather_c(1)
    gather_a(2)
    contract(0)
    back_1(0)
    gather_b(2)
    gather_d(1)
    dispatch(1)
    back_2(0)
    expand(1)
    gather_c(2)
    gather_a(3)
    contract(1)
    back_1(1)
    back_3(0)
    gather_b(3)
    gather_d(2)
    dispatch(2)
    back_2(1)
    expand(2)
    gather_c(3)
    back_4(0)
    contract(2)
    back_1(2)
    back_3(1)
    gather_d(3)
    dispatch(3)
    back_2(2)
    expand(3)
    back_4(1)
    contract(3)
    back_1(3)
    back_3(2)
    back_2(3)
    back_4(2)
    back_3(3)
    back_4(3)
    total = held[z, c, own, :, features].astype(F32)
    for k in range(1, spots):
        back_line(k).wait_recv()
        total = total + from_line[k - 1].astype(F32)
    out_ref[...] = total.astype(BF16)
    for k in range(1, spots):
        to_line(k).wait_send()
        back_line(k).wait_send()
    for k in range(spots):
        back_core(k).wait_send()
        back_second(k, 0).wait_send()
        back_second(k, 1).wait_send()
        back_first(k).wait_send()


def shards_fused(tokens, expert_ids, gate_values, expert_gate, expert_up, expert_down):
    nodes = lax.axis_size("node")
    per_node = lax.axis_size("local")
    experts = nodes * per_node
    spots = per_node // 2
    tok_rows, width = tokens.shape
    ff = expert_gate.shape[2]
    cap = 2 * tok_rows * expert_ids.shape[1] // experts
    dma = pltpu.SemaphoreType.DMA
    vmem = pl.BlockSpec(memory_space=pltpu.VMEM)
    anywhere = pl.BlockSpec(memory_space=pl.ANY)
    wide = width + LANES
    return pl.pallas_call(
        functools.partial(fused, spots, experts, cap),
        out_shape=jax.ShapeDtypeStruct((tok_rows, width), BF16),
        in_specs=[anywhere, vmem, vmem, anywhere, anywhere, anywhere],
        out_specs=vmem,
        scratch_shapes=[
            pltpu.VMEM((spots, 2, 4, tok_rows, wide), BF16),
            pltpu.VMEM((tok_rows, wide), BF16),
            pltpu.VMEM((spots, 4, tok_rows, width), BF16),
            pltpu.VMEM((spots, 2, tok_rows, width), BF16),
            pltpu.VMEM((spots, tok_rows, width), BF16),
            pltpu.VMEM((spots - 1, tok_rows, width), BF16),
            pltpu.VMEM((width, ff), BF16),
            pltpu.VMEM((width, ff), BF16),
            pltpu.VMEM((ff, width), BF16),
            pltpu.VMEM((8 * cap, width), BF16),
            pltpu.VMEM((8 * cap, ff), BF16),
            pltpu.VMEM((2, 4 * tok_rows, 4 * cap), BF16),
            pltpu.VMEM((2, 4 * tok_rows, 4 * cap), BF16),
            dma((5,)),
            dma((spots - 1,)),
            dma((spots - 1,)),
            dma((spots,)),
            dma((spots,)),
            dma((spots, 2)),
            dma((spots, 2)),
            dma((spots, 4)),
            dma((spots, 4)),
            dma((spots,)),
            dma((spots,)),
            dma((spots, 2)),
            dma((spots, 2)),
            dma((spots,)),
            dma((spots,)),
            dma((spots - 1,)),
            dma((spots - 1,)),
        ],
        compiler_params=pltpu.CompilerParams(
            collective_id=0, has_side_effects=True, vmem_limit_bytes=60 * 1024 * 1024
        ),
        cost_estimate=pl.CostEstimate(
            flops=48 * experts * cap * width * ff // 8,
            bytes_accessed=6 * width * ff,
            transcendentals=experts * cap * ff,
        ),
    )(tokens, expert_ids, gate_values, expert_gate, expert_up, expert_down)


def solution(mesh):
    placed = (
        P(("node", "local"), None),
        P(("node", "local"), None),
        P(("node", "local"), None),
        P(("node", "local"), None, None),
        P(("node", "local"), None, None),
        P(("node", "local"), None, None),
    )
    nodes, per_node = mesh.shape["node"], mesh.shape["local"]
    shards = shards_fused if nodes == 4 and per_node == 8 else shards_all_to_all
    return jax.shard_map(
        shards, mesh=mesh, in_specs=placed, out_specs=P(("node", "local"), None), check_vma=False
    )
```

```python
import functools

import jax
import jax.numpy as jnp
from jax import lax
from jax.experimental import pallas as pl
from jax.experimental.pallas import tpu as pltpu
from jax.sharding import PartitionSpec as P

BF16 = jnp.bfloat16
F32 = jnp.float32
LANES = 128


def expert_rows(rows, w_gate, w_up, w_down):
    shape = rows.shape
    flat = rows.reshape(-1, shape[-1])
    gate_rows = jnp.dot(flat, w_gate, preferred_element_type=jnp.float32)
    up_rows = jnp.dot(flat, w_up, preferred_element_type=jnp.float32)
    hidden = (jax.nn.silu(gate_rows) * up_rows).astype(jnp.bfloat16)
    output = jnp.dot(hidden, w_down, preferred_element_type=jnp.float32).astype(jnp.bfloat16)
    return output.reshape(shape)


def shards_all_to_all(tokens, expert_ids, gate_values, expert_gate, expert_up, expert_down):
    nodes = lax.axis_size("node")
    per_node = lax.axis_size("local")
    experts = nodes * per_node
    tok_rows, width = tokens.shape
    top = expert_ids.shape[1]
    cap = 2 * tok_rows * top // experts
    w_gate = expert_gate[0]
    w_up = expert_up[0]
    w_down = expert_down[0]
    hits = (expert_ids[:, :, None] == jnp.arange(experts, dtype=jnp.int32)[None, None, :]).astype(
        jnp.int32
    )
    flat_hits = hits.reshape(tok_rows * top, experts)
    earlier = jnp.cumsum(flat_hits, axis=0) - flat_hits
    slot = jnp.sum(earlier * flat_hits, axis=1).reshape(tok_rows, top)
    position = expert_ids * cap + slot
    places = jnp.arange(experts * cap, dtype=jnp.int32)
    chosen = places[:, None, None] == position[None, :, :]
    dispatch = jnp.any(chosen, axis=2).astype(jnp.bfloat16)
    weights = jnp.sum(
        jnp.where(chosen, gate_values[None, :, :].astype(jnp.float32), jnp.float32(0.0)), axis=2
    )
    send = jnp.dot(dispatch, tokens, preferred_element_type=jnp.float32).astype(jnp.bfloat16)
    back = lax.all_to_all(
        expert_rows(
            lax.all_to_all(
                send.reshape(experts, cap, width),
                ("node", "local"),
                split_axis=0,
                concat_axis=0,
                tiled=True,
            ),
            w_gate,
            w_up,
            w_down,
        ),
        ("node", "local"),
        split_axis=0,
        concat_axis=0,
        tiled=True,
    )
    mix = weights.astype(jnp.bfloat16).reshape(nodes, per_node * cap, tok_rows)
    node_part = jnp.einsum(
        "nct,ncd->ntd",
        mix,
        back.reshape(nodes, per_node * cap, width),
        preferred_element_type=jnp.float32,
    ).astype(jnp.bfloat16)
    return jnp.sum(node_part.astype(jnp.float32), axis=0).astype(jnp.bfloat16)


PLAN = (
    ("ga", 0, 0),
    ("gb", 0, 0),
    ("zz", 2, 0),
    ("ga", 1, 0),
    ("gc", 0, 0),
    ("gc", 0, 1),
    ("gd", 0, 0),
    ("zz", 3, 0),
    ("D", 0, 0),
    ("E", 0, 0),
    ("E", 0, 1),
    ("E", 0, 2),
    ("E", 0, 3),
    ("C", 0, 0),
    ("gc", 1, 0),
    ("gb", 1, 0),
    ("ga", 2, 0),
    ("C", 0, 1),
    ("gb", 2, 0),
    ("gc", 1, 1),
    ("b2", 0, 0),
    ("gd", 1, 0),
    ("D", 1, 0),
    ("E", 1, 0),
    ("E", 1, 1),
    ("gc", 2, 1),
    ("ga", 3, 0),
    ("E", 1, 2),
    ("E", 1, 3),
    ("gc", 2, 0),
    ("C", 1, 0),
    ("b2", 0, 1),
    ("gb", 3, 0),
    ("C", 1, 1),
    ("gd", 2, 0),
    ("gc", 3, 0),
    ("D", 2, 0),
    ("b2", 1, 0),
    ("E", 2, 0),
    ("b2", 1, 1),
    ("E", 2, 1),
    ("E", 2, 2),
    ("b3", 1, 0),
    ("bq", 0, 0),
    ("E", 2, 3),
    ("gc", 3, 1),
    ("b3", 1, 1),
    ("bq", 0, 1),
    ("C", 2, 0),
    ("C", 2, 1),
    ("gd", 3, 0),
    ("b3", 0, 0),
    ("b4", 1, 1),
    ("D", 3, 0),
    ("b3", 0, 1),
    ("b2", 2, 0),
    ("b4", 0, 0),
    ("b4", 1, 0),
    ("E", 3, 0),
    ("b2", 2, 1),
    ("E", 3, 1),
    ("E", 3, 2),
    ("b3", 2, 0),
    ("E", 3, 3),
    ("C", 3, 0),
    ("b3", 2, 1),
    ("b4", 2, 0),
    ("b2", 3, 0),
    ("b4", 2, 1),
    ("C", 3, 1),
    ("b3", 3, 0),
    ("b4", 0, 1),
    ("b2", 3, 1),
    ("b3", 3, 1),
    ("b4", 3, 0),
    ("b4", 3, 1),
)


def column_parts(width):
    tiles = width // 512
    lead = (tiles + 1) // 2 * 512
    return ((0, lead), (lead, width - lead))


def fused(
    spots,
    experts,
    cap,
    tok_ref,
    ids_ref,
    gates_ref,
    gate_hbm,
    up_hbm,
    down_hbm,
    out_ref,
    held,
    mine,
    spare,
    from_core,
    from_second,
    from_first,
    from_line,
    from_corner,
    w_gate,
    w_up,
    w_down,
    rows,
    hidden,
    pick,
    blend,
    local_sem,
    line_s,
    line_r,
    first_s,
    first_r,
    second_s,
    second_r,
    core_s,
    core_r,
    back_core_s,
    back_core_r,
    back_second_s,
    back_second_r,
    back_first_s,
    back_first_r,
    back_line_s,
    back_line_r,
    corner_s,
    corner_r,
    back_corner_s,
    back_corner_r,
):
    tok_rows, width = tok_ref.shape
    ff = w_gate.shape[1]
    quad = 4 * tok_rows
    columns = column_parts(width)
    slots = 4 * cap
    node = lax.axis_index("node")
    local = lax.axis_index("local")
    expert = node * (2 * spots) + local
    y, c, z, x = node // 2, node % 2, local // 2, local % 2
    a, b = x + c * (y - x), y + c * (x - y)
    step_a, step_b = 1 + c, 2 - c

    def q(i, j):
        return i * step_a + j * step_b

    def q_core(i, j):
        return i * step_b + j * step_a

    own, far = q(a, b), q(1 - a, 1 - b)
    order = ((a, b), (1 - a, b), (a, 1 - b), (1 - a, 1 - b))
    order_core = ((b, a), (1 - b, a), (b, 1 - a), (1 - b, 1 - a))
    first = ((y + c * (1 - 2 * y)) * 2 + c, z * 2 + x + (1 - c) * (1 - 2 * x))
    second = ((y + (1 - c) * (1 - 2 * y)) * 2 + c, z * 2 + x + c * (1 - 2 * x))
    sibling = (y * 2 + 1 - c, local)

    def along(k):
        return (node, ((z + k) % spots) * 2 + x)

    def spot(k):
        return (z + spots - k) % spots

    barrier = pltpu.get_barrier_semaphore()
    partners = [first, second, sibling] + [along(k) for k in range(1, spots)]
    for partner in partners:
        pl.semaphore_signal(
            barrier, inc=1, device_id=partner, device_id_type=pl.DeviceIdType.MESH
        )

    loads = [
        pltpu.make_async_copy(tok_ref, mine.at[:, pl.ds(0, width)], local_sem.at[0]),
        pltpu.make_async_copy(gate_hbm.at[0], w_gate, local_sem.at[1]),
        pltpu.make_async_copy(up_hbm.at[0], w_up, local_sem.at[2]),
        pltpu.make_async_copy(down_hbm.at[0], w_down, local_sem.at[3]),
    ]
    for load in loads:
        load.start()

    lane = lax.broadcasted_iota(jnp.int32, (LANES, tok_rows), 0)
    weight = jnp.zeros((LANES, tok_rows), F32)
    hit = jnp.zeros((LANES, tok_rows), F32)
    for k in range(ids_ref.shape[0]):
        chosen = ids_ref[k : k + 1, :]
        value = gates_ref[k : k + 1, :].astype(F32)
        weight = weight + jnp.where(lane == chosen, value, 0.0)
        hit = hit + jnp.where(lane == chosen + experts, 1.0, 0.0)
    earlier = (
        lax.broadcasted_iota(jnp.int32, (tok_rows, tok_rows), 0)
        < lax.broadcasted_iota(jnp.int32, (tok_rows, tok_rows), 1)
    )
    before = jnp.dot(
        hit.astype(BF16), jnp.where(earlier, 1.0, 0.0).astype(BF16), preferred_element_type=F32
    )
    notes = jnp.transpose(weight + hit * (before + 1.0))
    mine[:, pl.ds(width, LANES)] = notes.astype(BF16)
    loads[0].wait()
    keep = pltpu.make_async_copy(mine, held.at[z, c, own], local_sem.at[4])
    keep.start()
    pl.semaphore_wait(barrier, len(partners))

    def send(src, dst, send_sem, recv_sem, device):
        return pltpu.make_async_remote_copy(
            src_ref=src,
            dst_ref=dst,
            send_sem=send_sem,
            recv_sem=recv_sem,
            device_id=device,
            device_id_type=pl.DeviceIdType.MESH,
        )

    def block(k, i):
        return held.at[spot(k), c, q(*order[i])]

    def source(k, i):
        return mine if k == 0 and i == 0 else block(k, i)

    def to_line(k):
        return send(mine, held.at[z, c, own], line_s.at[k - 1], line_r.at[k - 1], along(k))

    def to_first(k):
        return send(source(k, 0), block(k, 0), first_s.at[k], first_r.at[k], first)

    def to_second(k, i):
        return send(source(k, i), block(k, i), second_s.at[k, i], second_r.at[k, i], second)

    def to_core(k, i):
        return send(source(k, i), block(k, i), core_s.at[k, i], core_r.at[k, i], sibling)

    def gather_a(k):
        if k > 0:
            send(mine, block(k, 0), line_s.at[k - 1], line_r.at[k - 1], along(k)).wait_recv()
        to_first(k).start()
        to_second(k, 0).start()
        to_core(k, 0).start()
        if k == 0:
            to_line(1).start()

    def gather_b(k):
        send(mine, block(k, 1), first_s.at[k], first_r.at[k], first).wait_recv()
        if k != 1:
            to_second(k, 1).start()
        to_core(k, 1).start()

    def corner():
        return send(spare, held.at[z, c, far], corner_s.at[0], corner_r.at[0], along(1))

    def gather_c(k, i):
        if k == 1 and i == 1:
            send(spare, block(1, 3), corner_s.at[0], corner_r.at[0], along(1)).wait_recv()
        else:
            send(
                mine, block(k, 2 + i), second_s.at[k, i], second_r.at[k, i], second
            ).wait_recv()
        to_core(k, 2 + i).start()
        if k == 0 and i == 1:
            copy = pltpu.make_async_copy(block(0, 3), spare, local_sem.at[5])
            copy.start()
            copy.wait()
            corner().start()

    def gather_d(k):
        for i in range(4):
            place = held.at[spot(k), 1 - c, q_core(*order_core[i])]
            send(mine, place, core_s.at[k, i], core_r.at[k, i], sibling).wait_recv()

    def gather_sent(k):
        to_first(k).wait_send()
        for i in range(1 if k == 1 else 2):
            to_second(k, i).wait_send()
        for i in range(4):
            to_core(k, i).wait_send()

    def dispatch(k):
        s = spot(k)
        lane = lax.broadcasted_iota(jnp.int32, (quad, LANES), 1)
        base = (lax.broadcasted_iota(jnp.int32, (quad, 1), 0) // tok_rows * cap).astype(F32)
        column = lax.broadcasted_iota(jnp.int32, (quad, slots), 1).astype(F32)
        for h in range(2):
            notes = held[s, h, :, :, pl.ds(width, LANES)].reshape(quad, LANES).astype(F32)
            weight = jnp.sum(jnp.where(lane == expert, notes, 0.0), axis=1, keepdims=True)
            place = jnp.sum(
                jnp.where(lane == expert + experts, notes, 0.0), axis=1, keepdims=True
            )
            target = jnp.where(place > 0.0, place - 1.0 + base, -1.0)
            pick[h] = jnp.transpose(jnp.where(column == target, 1.0, 0.0)).astype(BF16)
            blend[h] = jnp.where(column == target, weight, 0.0).astype(BF16)

        def piece(j, carry):
            cols = pl.ds(pl.multiple_of(j * 512, 512), 512)
            for h in range(2):
                rows[pl.ds(h * slots, slots), cols] = jnp.dot(
                    pick[h],
                    held[s, h, :, :, cols].reshape(quad, 512),
                    preferred_element_type=F32,
                ).astype(BF16)
            return carry

        lax.fori_loop(0, width // 512, piece, 0)

    def expand(k, part):
        if k == 0 and part == 0:
            loads[1].wait()
            loads[2].wait()

        tile = ff // 4
        cols = pl.ds(part * tile, tile)
        gate = jnp.dot(rows[...], w_gate[:, cols], preferred_element_type=F32)
        up = jnp.dot(rows[...], w_up[:, cols], preferred_element_type=F32)
        hidden[:, cols] = (gate / (1.0 + jnp.exp(-gate)) * up).astype(BF16)

    def contract(k, part):
        s = spot(k)
        if part == 0:
            if k == 0:
                loads[3].wait()
            gather_sent(k)

        def piece(j, carry):
            cols = pl.ds(pl.multiple_of(j * 512, 512), 512)
            made = jnp.dot(hidden[...], w_down[:, cols], preferred_element_type=F32).astype(BF16)
            for h in range(2):
                held[s, h, :, :, cols] = (
                    jnp.dot(
                        blend[h], made[h * slots : (h + 1) * slots], preferred_element_type=F32
                    )
                    .astype(BF16)
                    .reshape(4, tok_rows, 512)
                )
            return carry

        start, size = columns[part]
        lax.fori_loop(start // 512, (start + size) // 512, piece, 0)
        back_core(k, part).start()

    def span(part):
        start, size = columns[part]
        return pl.ds(start, size)

    def back_core(k, part):
        return send(
            held.at[spot(k), 1 - c, :, :, span(part)],
            from_core.at[k, :, :, span(part)],
            back_core_s.at[k, part],
            back_core_r.at[k, part],
            sibling,
        )

    def back_second(k, i, part):
        return send(
            held.at[spot(k), c, q(*order[2 + i]), :, span(part)],
            from_second.at[k, i, :, span(part)],
            back_second_s.at[k, i, part],
            back_second_r.at[k, i, part],
            second,
        )

    def back_corner(part):
        return send(
            held.at[spot(1), c, far, :, span(part)],
            from_corner.at[:, span(part)],
            back_corner_s.at[part],
            back_corner_r.at[part],
            (node, spot(1) * 2 + x),
        )

    def back_first(k, part):
        return send(
            held.at[spot(k), c, q(1 - a, b), :, span(part)],
            from_first.at[k, :, span(part)],
            back_first_s.at[k, part],
            back_first_r.at[k, part],
            first,
        )

    def back_line(k, part):
        return send(
            held.at[spot(k), c, own, :, span(part)],
            from_line.at[k - 1, :, span(part)],
            back_line_s.at[k - 1, part],
            back_line_r.at[k - 1, part],
            (node, spot(k) * 2 + x),
        )

    def add(k, place, part, other):
        cols = span(part)
        held[spot(k), c, place, :, cols] = (
            held[spot(k), c, place, :, cols].astype(F32) + other.astype(F32)
        ).astype(BF16)

    def back_2(k, part):
        cols = span(part)
        back_core(k, part).wait_recv()
        add(k, q(a, 1 - b), part, from_core[k, q(a, 1 - b), :, cols])
        back_second(k, 0, part).start()
        add(k, far, part, from_core[k, far, :, cols])
        if k == 1:
            back_corner(part).start()
        elif k > 1:
            back_second(k, 1, part).start()
        add(k, q(1 - a, b), part, from_core[k, q(1 - a, b), :, cols])
        add(k, own, part, from_core[k, own, :, cols])

    def back_far(part):
        back_corner(part).wait_recv()
        add(0, far, part, from_corner[:, span(part)])
        back_second(0, 1, part).start()

    def back_3(k, part):
        cols = span(part)
        back_second(k, 0, part).wait_recv()
        if k != 1:
            back_second(k, 1, part).wait_recv()
            add(k, q(1 - a, b), part, from_second[k, 1, :, cols])
        back_first(k, part).start()
        add(k, own, part, from_second[k, 0, :, cols])

    def back_4(k, part):
        back_first(k, part).wait_recv()
        add(k, own, part, from_first[k, :, span(part)])
        if k > 0:
            back_line(k, part).start()

    steps = {
        "ga": lambda k, i: gather_a(k),
        "zz": lambda k, i: to_line(k).start(),
        "gb": lambda k, i: gather_b(k),
        "gc": gather_c,
        "gd": lambda k, i: gather_d(k),
        "D": lambda k, i: dispatch(k),
        "E": expand,
        "C": contract,
        "b2": back_2,
        "bq": lambda k, i: back_far(i),
        "b3": back_3,
        "b4": back_4,
    }
    for name, k, i in PLAN:
        if name == "D" and k == 0:
            keep.wait()
        steps[name](k, i)
    for part in range(len(columns)):
        cols = span(part)
        total = held[z, c, own, :, cols].astype(F32)
        for k in range(1, spots):
            back_line(k, part).wait_recv()
            total = total + from_line[k - 1, :, cols].astype(F32)
        out_ref[:, cols] = total.astype(BF16)
    for k in range(1, spots):
        to_line(k).wait_send()
    corner().wait_send()
    for part in range(len(columns)):
        back_corner(part).wait_send()
        for k in range(spots):
            back_core(k, part).wait_send()
            back_first(k, part).wait_send()
            back_second(k, 0, part).wait_send()
            if k != 1:
                back_second(k, 1, part).wait_send()
            if k > 0:
                back_line(k, part).wait_send()


def shards_fused(tokens, expert_ids, gate_values, expert_gate, expert_up, expert_down):
    nodes = lax.axis_size("node")
    per_node = lax.axis_size("local")
    experts = nodes * per_node
    spots = per_node // 2
    tok_rows, width = tokens.shape
    ff = expert_gate.shape[2]
    cap = 2 * tok_rows * expert_ids.shape[1] // experts
    dma = pltpu.SemaphoreType.DMA
    parts = len(column_parts(width))
    vmem = pl.BlockSpec(memory_space=pltpu.VMEM)
    anywhere = pl.BlockSpec(memory_space=pl.ANY)
    wide = width + LANES
    return pl.pallas_call(
        functools.partial(fused, spots, experts, cap),
        out_shape=jax.ShapeDtypeStruct((tok_rows, width), BF16),
        in_specs=[anywhere, vmem, vmem, anywhere, anywhere, anywhere],
        out_specs=vmem,
        scratch_shapes=[
            pltpu.VMEM((spots, 2, 4, tok_rows, wide), BF16),
            pltpu.VMEM((tok_rows, wide), BF16),
            pltpu.VMEM((tok_rows, wide), BF16),
            pltpu.VMEM((spots, 4, tok_rows, width), BF16),
            pltpu.VMEM((spots, 2, tok_rows, width), BF16),
            pltpu.VMEM((spots, tok_rows, width), BF16),
            pltpu.VMEM((spots - 1, tok_rows, width), BF16),
            pltpu.VMEM((tok_rows, width), BF16),
            pltpu.VMEM((width, ff), BF16),
            pltpu.VMEM((width, ff), BF16),
            pltpu.VMEM((ff, width), BF16),
            pltpu.VMEM((8 * cap, width), BF16),
            pltpu.VMEM((8 * cap, ff), BF16),
            pltpu.VMEM((2, 4 * cap, 4 * tok_rows), BF16),
            pltpu.VMEM((2, 4 * tok_rows, 4 * cap), BF16),
            dma((6,)),
            dma((spots - 1,)),
            dma((spots - 1,)),
            dma((spots,)),
            dma((spots,)),
            dma((spots, 2)),
            dma((spots, 2)),
            dma((spots, 4)),
            dma((spots, 4)),
            dma((spots, parts)),
            dma((spots, parts)),
            dma((spots, 2, parts)),
            dma((spots, 2, parts)),
            dma((spots, parts)),
            dma((spots, parts)),
            dma((spots - 1, parts)),
            dma((spots - 1, parts)),
            dma((1,)),
            dma((1,)),
            dma((parts,)),
            dma((parts,)),
        ],
        compiler_params=pltpu.CompilerParams(
            collective_id=0, has_side_effects=True, vmem_limit_bytes=60 * 1024 * 1024
        ),
        cost_estimate=pl.CostEstimate(
            flops=48 * experts * cap * width * ff // 8,
            bytes_accessed=6 * width * ff,
            transcendentals=experts * cap * ff,
        ),
    )(tokens, expert_ids.T, gate_values.T, expert_gate, expert_up, expert_down)


def solution(mesh):
    placed = (
        P(("node", "local"), None),
        P(("node", "local"), None),
        P(("node", "local"), None),
        P(("node", "local"), None, None),
        P(("node", "local"), None, None),
        P(("node", "local"), None, None),
    )
    nodes, per_node = mesh.shape["node"], mesh.shape["local"]
    shards = shards_fused if nodes == 4 and per_node == 8 else shards_all_to_all
    return jax.shard_map(
        shards, mesh=mesh, in_specs=placed, out_specs=P(("node", "local"), None), check_vma=False
    )
```

```python
import functools

import jax
import jax.numpy as jnp
from jax import lax
from jax.experimental import pallas as pl
from jax.experimental.pallas import tpu as pltpu
from jax.sharding import PartitionSpec as P

BF16 = jnp.bfloat16
F32 = jnp.float32
LANES = 128


def expert_rows(rows, w_gate, w_up, w_down):
    shape = rows.shape
    flat = rows.reshape(-1, shape[-1])
    gate_rows = jnp.dot(flat, w_gate, preferred_element_type=jnp.float32)
    up_rows = jnp.dot(flat, w_up, preferred_element_type=jnp.float32)
    hidden = (jax.nn.silu(gate_rows) * up_rows).astype(jnp.bfloat16)
    output = jnp.dot(hidden, w_down, preferred_element_type=jnp.float32).astype(jnp.bfloat16)
    return output.reshape(shape)


def shards_all_to_all(tokens, expert_ids, gate_values, expert_gate, expert_up, expert_down):
    nodes = lax.axis_size("node")
    per_node = lax.axis_size("local")
    experts = nodes * per_node
    tok_rows, width = tokens.shape
    top = expert_ids.shape[1]
    cap = 2 * tok_rows * top // experts
    w_gate = expert_gate[0]
    w_up = expert_up[0]
    w_down = expert_down[0]
    hits = (expert_ids[:, :, None] == jnp.arange(experts, dtype=jnp.int32)[None, None, :]).astype(
        jnp.int32
    )
    flat_hits = hits.reshape(tok_rows * top, experts)
    earlier = jnp.cumsum(flat_hits, axis=0) - flat_hits
    slot = jnp.sum(earlier * flat_hits, axis=1).reshape(tok_rows, top)
    position = expert_ids * cap + slot
    places = jnp.arange(experts * cap, dtype=jnp.int32)
    chosen = places[:, None, None] == position[None, :, :]
    dispatch = jnp.any(chosen, axis=2).astype(jnp.bfloat16)
    weights = jnp.sum(
        jnp.where(chosen, gate_values[None, :, :].astype(jnp.float32), jnp.float32(0.0)), axis=2
    )
    send = jnp.dot(dispatch, tokens, preferred_element_type=jnp.float32).astype(jnp.bfloat16)
    back = lax.all_to_all(
        expert_rows(
            lax.all_to_all(
                send.reshape(experts, cap, width),
                ("node", "local"),
                split_axis=0,
                concat_axis=0,
                tiled=True,
            ),
            w_gate,
            w_up,
            w_down,
        ),
        ("node", "local"),
        split_axis=0,
        concat_axis=0,
        tiled=True,
    )
    mix = weights.astype(jnp.bfloat16).reshape(nodes, per_node * cap, tok_rows)
    node_part = jnp.einsum(
        "nct,ncd->ntd",
        mix,
        back.reshape(nodes, per_node * cap, width),
        preferred_element_type=jnp.float32,
    ).astype(jnp.bfloat16)
    return jnp.sum(node_part.astype(jnp.float32), axis=0).astype(jnp.bfloat16)


PLAN = (
    ("ga", 0, 0),
    ("zz", 2, 0),
    ("gb", 0, 0),
    ("ga", 1, 0),
    ("gc", 0, 0),
    ("gc", 0, 1),
    ("zz", 3, 0),
    ("gd", 0, 0),
    ("D", 0, 0),
    ("E", 0, 0),
    ("E", 0, 1),
    ("C", 0, 0),
    ("ga", 2, 0),
    ("C", 0, 1),
    ("gc", 1, 0),
    ("gb", 1, 0),
    ("gc", 1, 1),
    ("gb", 2, 0),
    ("b2", 0, 1),
    ("b2", 0, 0),
    ("gd", 1, 0),
    ("D", 1, 0),
    ("gc", 2, 0),
    ("E", 1, 0),
    ("gc", 2, 1),
    ("E", 1, 1),
    ("ga", 3, 0),
    ("C", 1, 0),
    ("gd", 2, 0),
    ("C", 1, 1),
    ("b2", 1, 0),
    ("D", 2, 0),
    ("E", 2, 0),
    ("gb", 3, 0),
    ("bq", 0, 0),
    ("b2", 1, 1),
    ("E", 2, 1),
    ("b3", 1, 0),
    ("gc", 3, 0),
    ("gc", 3, 1),
    ("C", 2, 0),
    ("C", 2, 1),
    ("b3", 1, 1),
    ("gd", 3, 0),
    ("D", 3, 0),
    ("b2", 2, 0),
    ("b2", 2, 1),
    ("b4", 1, 0),
    ("b4", 1, 1),
    ("E", 3, 0),
    ("b3", 2, 0),
    ("E", 3, 1),
    ("b3", 2, 1),
    ("b3", 0, 0),
    ("bq", 0, 1),
    ("b4", 2, 0),
    ("C", 3, 0),
    ("C", 3, 1),
    ("b2", 3, 0),
    ("b4", 2, 1),
    ("b3", 3, 0),
    ("b2", 3, 1),
    ("b4", 3, 0),
    ("b3", 0, 1),
    ("b3", 3, 1),
    ("b4", 0, 1),
    ("b4", 3, 1),
    ("b4", 0, 0),
)


def column_parts(width):
    tiles = width // 512
    lead = (tiles + 1) // 2 * 512
    return ((0, lead), (lead, width - lead))


def fused(
    spots,
    experts,
    cap,
    tok_ref,
    ids_ref,
    gates_ref,
    gate_hbm,
    up_hbm,
    down_hbm,
    out_ref,
    held,
    mine,
    spare,
    from_core,
    from_second,
    from_first,
    from_line,
    from_corner,
    w_gate,
    w_up,
    w_down,
    rows,
    hidden,
    pick,
    blend,
    local_sem,
    line_s,
    line_r,
    first_s,
    first_r,
    second_s,
    second_r,
    core_s,
    core_r,
    back_core_s,
    back_core_r,
    back_second_s,
    back_second_r,
    back_first_s,
    back_first_r,
    back_line_s,
    back_line_r,
    corner_s,
    corner_r,
    back_corner_s,
    back_corner_r,
):
    tok_rows, width = tok_ref.shape
    ff = w_gate.shape[1]
    quad = 4 * tok_rows
    columns = column_parts(width)
    slots = 4 * cap
    node = lax.axis_index("node")
    local = lax.axis_index("local")
    expert = node * (2 * spots) + local
    y, c, z, x = node // 2, node % 2, local // 2, local % 2
    a, b = x + c * (y - x), y + c * (x - y)
    step_a, step_b = 1 + c, 2 - c

    def q(i, j):
        return i * step_a + j * step_b

    def q_core(i, j):
        return i * step_b + j * step_a

    own, far = q(a, b), q(1 - a, 1 - b)
    order = ((a, b), (1 - a, b), (a, 1 - b), (1 - a, 1 - b))
    order_core = ((b, a), (1 - b, a), (b, 1 - a), (1 - b, 1 - a))
    first = ((y + c * (1 - 2 * y)) * 2 + c, z * 2 + x + (1 - c) * (1 - 2 * x))
    second = ((y + (1 - c) * (1 - 2 * y)) * 2 + c, z * 2 + x + c * (1 - 2 * x))
    sibling = (y * 2 + 1 - c, local)

    def along(k):
        return (node, ((z + k) % spots) * 2 + x)

    def spot(k):
        return (z + spots - k) % spots

    barrier = pltpu.get_barrier_semaphore()
    partners = [first, second, sibling] + [along(k) for k in range(1, spots)]
    for partner in partners:
        pl.semaphore_signal(
            barrier, inc=1, device_id=partner, device_id_type=pl.DeviceIdType.MESH
        )

    loads = [
        pltpu.make_async_copy(tok_ref, mine.at[:, pl.ds(0, width)], local_sem.at[0]),
        pltpu.make_async_copy(gate_hbm.at[0], w_gate, local_sem.at[1]),
        pltpu.make_async_copy(up_hbm.at[0], w_up, local_sem.at[2]),
        pltpu.make_async_copy(down_hbm.at[0], w_down, local_sem.at[3]),
    ]
    for load in loads:
        load.start()

    lane = lax.broadcasted_iota(jnp.int32, (LANES, tok_rows), 0)
    weight = jnp.zeros((LANES, tok_rows), F32)
    hit = jnp.zeros((LANES, tok_rows), F32)
    for k in range(ids_ref.shape[0]):
        chosen = ids_ref[k : k + 1, :]
        value = gates_ref[k : k + 1, :].astype(F32)
        weight = weight + jnp.where(lane == chosen, value, 0.0)
        hit = hit + jnp.where(lane == chosen + experts, 1.0, 0.0)
    earlier = (
        lax.broadcasted_iota(jnp.int32, (tok_rows, tok_rows), 0)
        < lax.broadcasted_iota(jnp.int32, (tok_rows, tok_rows), 1)
    )
    before = jnp.dot(
        hit.astype(BF16), jnp.where(earlier, 1.0, 0.0).astype(BF16), preferred_element_type=F32
    )
    notes = jnp.transpose(weight + hit * (before + 1.0))
    mine[:, pl.ds(width, LANES)] = notes.astype(BF16)
    loads[0].wait()
    keep = pltpu.make_async_copy(mine, held.at[z, c, own], local_sem.at[4])
    keep.start()
    pl.semaphore_wait(barrier, len(partners))

    def send(src, dst, send_sem, recv_sem, device):
        return pltpu.make_async_remote_copy(
            src_ref=src,
            dst_ref=dst,
            send_sem=send_sem,
            recv_sem=recv_sem,
            device_id=device,
            device_id_type=pl.DeviceIdType.MESH,
        )

    def block(k, i):
        return held.at[spot(k), c, q(*order[i])]

    def source(k, i):
        return mine if k == 0 and i == 0 else block(k, i)

    def to_line(k):
        return send(mine, held.at[z, c, own], line_s.at[k - 1], line_r.at[k - 1], along(k))

    def to_first(k):
        return send(source(k, 0), block(k, 0), first_s.at[k], first_r.at[k], first)

    def to_second(k, i):
        return send(source(k, i), block(k, i), second_s.at[k, i], second_r.at[k, i], second)

    def to_core(k, i):
        return send(source(k, i), block(k, i), core_s.at[k, i], core_r.at[k, i], sibling)

    def gather_a(k):
        if k > 0:
            send(mine, block(k, 0), line_s.at[k - 1], line_r.at[k - 1], along(k)).wait_recv()
        to_first(k).start()
        to_second(k, 0).start()
        to_core(k, 0).start()
        if k == 0:
            to_line(1).start()

    def gather_b(k):
        send(mine, block(k, 1), first_s.at[k], first_r.at[k], first).wait_recv()
        if k != 1:
            to_second(k, 1).start()
        to_core(k, 1).start()

    def corner():
        return send(spare, held.at[z, c, far], corner_s.at[0], corner_r.at[0], along(1))

    def gather_c(k, i):
        if k == 1 and i == 1:
            send(spare, block(1, 3), corner_s.at[0], corner_r.at[0], along(1)).wait_recv()
        else:
            send(
                mine, block(k, 2 + i), second_s.at[k, i], second_r.at[k, i], second
            ).wait_recv()
        to_core(k, 2 + i).start()
        if k == 0 and i == 1:
            copy = pltpu.make_async_copy(block(0, 3), spare, local_sem.at[5])
            copy.start()
            copy.wait()
            corner().start()

    def gather_d(k):
        for i in range(4):
            place = held.at[spot(k), 1 - c, q_core(*order_core[i])]
            send(mine, place, core_s.at[k, i], core_r.at[k, i], sibling).wait_recv()

    def gather_sent(k):
        to_first(k).wait_send()
        for i in range(1 if k == 1 else 2):
            to_second(k, i).wait_send()
        for i in range(4):
            to_core(k, i).wait_send()

    def dispatch(k):
        s = spot(k)
        lane = lax.broadcasted_iota(jnp.int32, (quad, LANES), 1)
        base = (lax.broadcasted_iota(jnp.int32, (quad, 1), 0) // tok_rows * cap).astype(F32)
        column = lax.broadcasted_iota(jnp.int32, (quad, slots), 1).astype(F32)
        for h in range(2):
            notes = held[s, h, :, :, pl.ds(width, LANES)].reshape(quad, LANES).astype(F32)
            weight = jnp.sum(jnp.where(lane == expert, notes, 0.0), axis=1, keepdims=True)
            place = jnp.sum(
                jnp.where(lane == expert + experts, notes, 0.0), axis=1, keepdims=True
            )
            target = jnp.where(place > 0.0, place - 1.0 + base, -1.0)
            pick[h] = jnp.transpose(jnp.where(column == target, 1.0, 0.0)).astype(BF16)
            blend[h] = jnp.where(column == target, weight, 0.0).astype(BF16)

        for j in range(width // 512):
            cols = pl.ds(j * 512, 512)
            for h in range(2):
                rows[pl.ds(h * slots, slots), cols] = jnp.dot(
                    pick[h],
                    held[s, h, :, :, cols].reshape(quad, 512),
                    preferred_element_type=F32,
                ).astype(BF16)

    def expand(k, part):
        if k == 0 and part == 0:
            loads[1].wait()
            loads[2].wait()

        tile = ff // 2
        cols = pl.ds(part * tile, tile)
        gate = jnp.dot(rows[...], w_gate[:, cols], preferred_element_type=F32)
        up = jnp.dot(rows[...], w_up[:, cols], preferred_element_type=F32)
        hidden[:, cols] = (gate / (1.0 + jnp.exp(-gate)) * up).astype(BF16)

    def contract(k, part):
        s = spot(k)
        if part == 0:
            if k == 0:
                loads[3].wait()
            gather_sent(k)

        start, size = columns[part]
        for j in range(start // 512, (start + size) // 512):
            cols = pl.ds(j * 512, 512)
            made = jnp.dot(hidden[...], w_down[:, cols], preferred_element_type=F32).astype(BF16)
            for h in range(2):
                held[s, h, :, :, cols] = (
                    jnp.dot(
                        blend[h], made[h * slots : (h + 1) * slots], preferred_element_type=F32
                    )
                    .astype(BF16)
                    .reshape(4, tok_rows, 512)
                )
        back_core(k, part).start()

    def span(part):
        start, size = columns[part]
        return pl.ds(start, size)

    def back_core(k, part):
        return send(
            held.at[spot(k), 1 - c, :, :, span(part)],
            from_core.at[k, :, :, span(part)],
            back_core_s.at[k, part],
            back_core_r.at[k, part],
            sibling,
        )

    def back_second(k, i, part):
        return send(
            held.at[spot(k), c, q(*order[2 + i]), :, span(part)],
            from_second.at[k, i, :, span(part)],
            back_second_s.at[k, i, part],
            back_second_r.at[k, i, part],
            second,
        )

    def back_corner(part):
        return send(
            held.at[spot(1), c, far, :, span(part)],
            from_corner.at[:, span(part)],
            back_corner_s.at[part],
            back_corner_r.at[part],
            (node, spot(1) * 2 + x),
        )

    def back_first(k, part):
        return send(
            held.at[spot(k), c, q(1 - a, b), :, span(part)],
            from_first.at[k, :, span(part)],
            back_first_s.at[k, part],
            back_first_r.at[k, part],
            first,
        )

    def back_line(k, part):
        return send(
            held.at[spot(k), c, own, :, span(part)],
            from_line.at[k - 1, :, span(part)],
            back_line_s.at[k - 1, part],
            back_line_r.at[k - 1, part],
            (node, spot(k) * 2 + x),
        )

    def add(k, place, part, other):
        cols = span(part)
        held[spot(k), c, place, :, cols] = (
            held[spot(k), c, place, :, cols].astype(F32) + other.astype(F32)
        ).astype(BF16)

    def back_2(k, part):
        cols = span(part)
        back_core(k, part).wait_recv()
        add(k, q(a, 1 - b), part, from_core[k, q(a, 1 - b), :, cols])
        back_second(k, 0, part).start()
        add(k, far, part, from_core[k, far, :, cols])
        if k == 1:
            back_corner(part).start()
        elif k > 1:
            back_second(k, 1, part).start()
        add(k, q(1 - a, b), part, from_core[k, q(1 - a, b), :, cols])
        add(k, own, part, from_core[k, own, :, cols])

    def back_far(part):
        back_corner(part).wait_recv()
        add(0, far, part, from_corner[:, span(part)])
        back_second(0, 1, part).start()

    def back_3(k, part):
        cols = span(part)
        back_second(k, 0, part).wait_recv()
        if k != 1:
            back_second(k, 1, part).wait_recv()
            add(k, q(1 - a, b), part, from_second[k, 1, :, cols])
        back_first(k, part).start()
        add(k, own, part, from_second[k, 0, :, cols])

    def back_4(k, part):
        back_first(k, part).wait_recv()
        add(k, own, part, from_first[k, :, span(part)])
        if k > 0:
            back_line(k, part).start()

    steps = {
        "ga": lambda k, i: gather_a(k),
        "zz": lambda k, i: to_line(k).start(),
        "gb": lambda k, i: gather_b(k),
        "gc": gather_c,
        "gd": lambda k, i: gather_d(k),
        "D": lambda k, i: dispatch(k),
        "E": expand,
        "C": contract,
        "b2": back_2,
        "bq": lambda k, i: back_far(i),
        "b3": back_3,
        "b4": back_4,
    }
    for name, k, i in PLAN:
        if name == "D" and k == 0:
            keep.wait()
        steps[name](k, i)
    for part in range(len(columns)):
        cols = span(part)
        total = held[z, c, own, :, cols].astype(F32)
        for k in range(1, spots):
            back_line(k, part).wait_recv()
            total = total + from_line[k - 1, :, cols].astype(F32)
        out_ref[:, cols] = total.astype(BF16)
    for k in range(1, spots):
        to_line(k).wait_send()
    corner().wait_send()
    for part in range(len(columns)):
        back_corner(part).wait_send()
        for k in range(spots):
            back_core(k, part).wait_send()
            back_first(k, part).wait_send()
            back_second(k, 0, part).wait_send()
            if k != 1:
                back_second(k, 1, part).wait_send()
            if k > 0:
                back_line(k, part).wait_send()


def shards_fused(tokens, expert_ids, gate_values, expert_gate, expert_up, expert_down):
    nodes = lax.axis_size("node")
    per_node = lax.axis_size("local")
    experts = nodes * per_node
    spots = per_node // 2
    tok_rows, width = tokens.shape
    ff = expert_gate.shape[2]
    cap = 2 * tok_rows * expert_ids.shape[1] // experts
    dma = pltpu.SemaphoreType.DMA
    parts = len(column_parts(width))
    vmem = pl.BlockSpec(memory_space=pltpu.VMEM)
    anywhere = pl.BlockSpec(memory_space=pl.ANY)
    wide = width + LANES
    return pl.pallas_call(
        functools.partial(fused, spots, experts, cap),
        out_shape=jax.ShapeDtypeStruct((tok_rows, width), BF16),
        in_specs=[anywhere, vmem, vmem, anywhere, anywhere, anywhere],
        out_specs=vmem,
        scratch_shapes=[
            pltpu.VMEM((spots, 2, 4, tok_rows, wide), BF16),
            pltpu.VMEM((tok_rows, wide), BF16),
            pltpu.VMEM((tok_rows, wide), BF16),
            pltpu.VMEM((spots, 4, tok_rows, width), BF16),
            pltpu.VMEM((spots, 2, tok_rows, width), BF16),
            pltpu.VMEM((spots, tok_rows, width), BF16),
            pltpu.VMEM((spots - 1, tok_rows, width), BF16),
            pltpu.VMEM((tok_rows, width), BF16),
            pltpu.VMEM((width, ff), BF16),
            pltpu.VMEM((width, ff), BF16),
            pltpu.VMEM((ff, width), BF16),
            pltpu.VMEM((8 * cap, width), BF16),
            pltpu.VMEM((8 * cap, ff), BF16),
            pltpu.VMEM((2, 4 * cap, 4 * tok_rows), BF16),
            pltpu.VMEM((2, 4 * tok_rows, 4 * cap), BF16),
            dma((6,)),
            dma((spots - 1,)),
            dma((spots - 1,)),
            dma((spots,)),
            dma((spots,)),
            dma((spots, 2)),
            dma((spots, 2)),
            dma((spots, 4)),
            dma((spots, 4)),
            dma((spots, parts)),
            dma((spots, parts)),
            dma((spots, 2, parts)),
            dma((spots, 2, parts)),
            dma((spots, parts)),
            dma((spots, parts)),
            dma((spots - 1, parts)),
            dma((spots - 1, parts)),
            dma((1,)),
            dma((1,)),
            dma((parts,)),
            dma((parts,)),
        ],
        compiler_params=pltpu.CompilerParams(
            collective_id=0, has_side_effects=True, vmem_limit_bytes=60 * 1024 * 1024
        ),
        cost_estimate=pl.CostEstimate(
            flops=48 * experts * cap * width * ff // 8,
            bytes_accessed=6 * width * ff,
            transcendentals=experts * cap * ff,
        ),
    )(tokens, expert_ids.T, gate_values.T, expert_gate, expert_up, expert_down)


def solution(mesh):
    placed = (
        P(("node", "local"), None),
        P(("node", "local"), None),
        P(("node", "local"), None),
        P(("node", "local"), None, None),
        P(("node", "local"), None, None),
        P(("node", "local"), None, None),
    )
    nodes, per_node = mesh.shape["node"], mesh.shape["local"]
    shards = shards_fused if nodes == 4 and per_node == 8 else shards_all_to_all
    return jax.shard_map(
        shards, mesh=mesh, in_specs=placed, out_specs=P(("node", "local"), None), check_vma=False
    )
```
